256 devices in a mesh: wide: 64 (over y, x, z_hi), narrow: 4 (over z_lo, core).
Axes of the slice: x: 4, y: 4, z: 8 (z_hi: 4, z_lo: 2; z = z_hi * 2 + z_lo), core: 2. Of those that a mesh axis runs over, the one named last changes fastest.
Arguments:
- target_position: float32 [3, 16384], P(None, ('wide', 'narrow')), may hold values from 0 to 4
- target_vector: float32 [3, 16384], P(None, ('wide', 'narrow')), may hold values from -4 to 4
- target_radius: float32 [16384], P(('wide', 'narrow')), may hold values from 0.05 to 0.5
- source_position: float32 [3, 262144], P(None, ('wide', 'narrow')), may hold values from 0 to 4
- source_vector: float32 [3, 262144], P(None, ('wide', 'narrow')), may hold values from -4 to 4
- source_radius: float32 [262144], P(('wide', 'narrow')), may hold values from 0.05 to 0.5
- source_current: float32 [262144], P(('wide', 'narrow')), may hold values from -0.125 to 0.125
- incidence: int32 [262144], P(('wide', 'narrow')), may hold values from 0 to 127
- excitation: int32 [128], replicated, may hold values from 0 to 127, each once
Outputs:
- voltages: float32 [16384, 128], P(('wide', 'narrow'))
The draws below stay inside these ranges and needn't reach their ends.
Inputs may be any that keep to these rules, and one draw needn't show every extreme that they name: Each excitation column excites a different port.
All inputs are finite; a program needn't handle non-finite values.
Results may differ from the reference program's by a relative error of at most 0.0043.
Values sent between devices are 32-bit elements; how exact they have to be, the bound alone decides.
No kernel may reach another device: no remote copies, remote signals or barrier semaphores. Data moves between devices by JAX's collectives and lax.ppermute only.
A program may use at most 128 MiB of HBM per device.

```python
import math
import jax
import jax.numpy as jnp
from jax import lax

EXC = 128
NROW = 16384
NCOL = 262144


def plant(array, stream_key, least, top_value):
    extent = array.shape
    index_at = [jax.random.randint(jax.random.fold_in(stream_key, axis), (), 0, extent[axis]) for axis in range(len(extent))]
    array = array.at[tuple(index_at)].set(least)
    longest = extent.index(max(extent))
    index_at[longest] = (index_at[longest] + 1) % extent[longest]
    return array.at[tuple(index_at)].set(top_value)


def shard_levels(rng, dims, cuts, least, top_value):
    def one(position, parts):
        draws = jax.random.uniform(jax.random.fold_in(jax.random.fold_in(rng, 6), position), (parts,), jnp.float32, least / len(cuts), top_value / len(cuts))
        return jnp.repeat(jnp.exp(draws), dims[position] // parts).reshape((-1,) + (1,) * (len(dims) - position - 1))

    gain = one(*cuts[0])
    for cut in cuts[1:]:
        gain = gain * one(*cut)
    return gain


def bell_draw(stream_key, shape, width, bound, split=(), kind=jnp.bfloat16):
    drawn = jax.random.normal(stream_key, shape, jnp.float32) * width
    if len(split) > 0:
        drawn = shard_levels(stream_key, shape, split, -0.22, 0.18) * drawn
    return jnp.clip(drawn, min=-bound, max=bound).astype(kind)


def setup_inputs(seed: int = 0) -> dict:
    keys = jax.random.split(jax.random.key(seed), 10)
    return {
        "target_position": jnp.clip(4.0 * jax.random.uniform(keys[0], (3, NROW), jnp.float32) ** shard_levels(keys[0], (3, NROW), ((1, 256),), -0.2, 0.2), 0.0, 4.0),
        "target_vector": bell_draw(keys[1], (3, NROW), 1.0, 4.0, ((1, 256),), jnp.float32),
        "target_radius": jnp.clip(jnp.exp(math.log(0.5) - 2.3025851 * jax.random.uniform(keys[2], (NROW,), jnp.float32) ** shard_levels(keys[2], (NROW,), ((0, 256),), -0.2, 0.2)), 0.05, 0.5),
        "source_position": jnp.clip(4.0 * jax.random.uniform(keys[3], (3, NCOL), jnp.float32) ** shard_levels(keys[3], (3, NCOL), ((1, 256),), -0.2, 0.2), 0.0, 4.0),
        "source_vector": bell_draw(keys[4], (3, NCOL), 1.0, 4.0, ((1, 256),), jnp.float32),
        "source_radius": jnp.clip(jnp.exp(math.log(0.5) - 2.3025851 * jax.random.uniform(keys[5], (NCOL,), jnp.float32) ** shard_levels(keys[5], (NCOL,), ((0, 256),), -0.2, 0.2)), 0.05, 0.5),
        "source_current": bell_draw(keys[6], (NCOL,), (NCOL // EXC) ** -0.5, 0.125, ((0, 256),), jnp.float32),
        "incidence": plant(jax.random.randint(keys[7], (NCOL,), 0, EXC), jax.random.fold_in(keys[7], 1), 0, EXC - 1).astype(jnp.int32),
        "excitation": jax.random.permutation(keys[8], EXC).astype(jnp.int32),
    }


def panel_block(targets, sources):
    delta_x = targets[0][:, None] - sources[0][None, :]
    delta_y = targets[1][:, None] - sources[1][None, :]
    delta_z = targets[2][:, None] - sources[2][None, :]
    reach = targets[6][:, None] + sources[6][None, :]
    distance = delta_x * delta_x + delta_y * delta_y + delta_z * delta_z + reach * reach
    alignment = targets[3][:, None] * sources[3][None, :] + targets[4][:, None] * sources[4][None, :] + targets[5][:, None] * sources[5][None, :]
    return (alignment * lax.rsqrt(distance)).astype(jnp.bfloat16)

def reference(target_position, target_vector, target_radius, source_position, source_vector, source_radius, source_current, incidence, excitation):
    matched = incidence[:, None] == excitation[None, :]
    currents = jnp.where(matched, source_current[:, None], jnp.zeros((), source_current.dtype)).astype(jnp.bfloat16)
    targets = jnp.concatenate([target_position, target_vector, target_radius[None, :]], 0)
    sources = jnp.concatenate([source_position, source_vector, source_radius[None, :]], 0)
    row_count = targets.shape[1]
    row_step = math.gcd(row_count, 128)
    stacked = targets.reshape(7, row_count // row_step, row_step).transpose(1, 0, 2)

    def one_step(slab_rows):
        return jnp.dot(panel_block(slab_rows, sources), currents, preferred_element_type=jnp.float32)
    return lax.map(one_step, stacked).reshape(row_count, currents.shape[1])
```

```python
import functools

import jax
import jax.numpy as jnp
from jax import lax
from jax.experimental import pallas as pl
from jax.experimental.pallas import tpu as pltpu
from jax.sharding import Mesh, PartitionSpec as P

BF16 = jnp.bfloat16
F32 = jnp.float32
DEPTH = 64
LANES = 128
AXES = ("y", "x", "zh", "zl", "c")
SHAPE = (4, 4, 4, 2, 2)


def split3(x):
    high = x.astype(BF16).astype(F32)
    rest = x - high
    middle = rest.astype(BF16).astype(F32)
    low = (rest - middle).astype(BF16).astype(F32)
    return high, middle, low


def centred(x):
    row = lax.broadcasted_iota(jnp.int32, x.shape, 0)
    x = jnp.where(row < 3, x - 2.0, x)
    norm = jnp.sum(jnp.where(row < 4, x * x, 0.0), axis=0, keepdims=True)
    return row, x, split3(norm)


def source_features(x):
    row, x, (n_high, n_middle, n_low) = centred(x)
    high, middle, low = split3(x)
    norms = jnp.where(
        row == 0,
        n_high,
        jnp.where(row == 1, n_middle, jnp.where(row == 2, n_low, jnp.where(row < 6, 1.0, 0.0))),
    )
    parts = [high, high, high, middle, middle, low, norms, jnp.zeros_like(x)]
    return jnp.concatenate(parts, 0).astype(BF16)


def target_features(x):
    row, x, (n_high, n_middle, n_low) = centred(x)
    high, middle, low = split3(x)
    norms = jnp.where(
        row < 3,
        1.0,
        jnp.where(row == 3, n_high, jnp.where(row == 4, n_middle, jnp.where(row == 5, n_low, 0.0))),
    )
    zero = jnp.zeros_like(x)

    def stack(weight, last):
        parts = [high, middle, low, high, middle, high]
        return jnp.concatenate([p * weight for p in parts] + [last, zero], 0)

    squared = stack(jnp.where(row < 3, -2.0, jnp.where(row == 3, 2.0, 0.0)), norms)
    aligned = stack(jnp.where((row >= 4) & (row < 7), 1.0, 0.0), zero)
    return squared, aligned


def volts_kernel(targets, sources, ports, out, squared, aligned, features, currents):
    blocks, count = targets.shape[0], targets.shape[2]
    width = features.shape[1]
    for i in range(blocks):
        here = slice(i * count, (i + 1) * count)
        d, a = target_features(targets[i])
        squared[here, :] = jnp.transpose(d).astype(BF16)
        aligned[here, :] = jnp.transpose(a).astype(BF16)
    out[...] = jnp.zeros_like(out)
    port = ports[...]

    def block(b, carry):
        for r in range(width // LANES):
            here = slice(r * LANES, (r + 1) * LANES)
            features[:, here] = source_features(sources[b, pl.ds(r, 8, stride=8), :])
            current = sources[b, pl.ds(56 + r, 1), :]
            incidence = sources[b, pl.ds(64 + r, 1), :]
            currents[:, here] = jnp.where(port == incidence, current, 0.0).astype(BF16)
        distance = jnp.dot(squared[...], features[...], preferred_element_type=F32)
        alignment = jnp.dot(aligned[...], features[...], preferred_element_type=F32)
        inductance = (alignment * lax.rsqrt(distance)).astype(BF16)
        out[...] += lax.dot_general(
            inductance, currents[...], (((1,), (1,)), ((), ())), preferred_element_type=F32
        )
        return carry

    lax.fori_loop(0, sources.shape[0], block, 0)


def volts(targets, sources, ports):
    rows = targets.shape[0] * targets.shape[2]
    width = sources.shape[1] // 9 * LANES
    vmem = pl.BlockSpec(memory_space=pltpu.VMEM)
    pairs = rows * sources.shape[0] * width
    return pl.pallas_call(
        volts_kernel,
        out_shape=jax.ShapeDtypeStruct((rows, ports.shape[0]), F32),
        in_specs=[vmem, vmem, vmem],
        out_specs=vmem,
        scratch_shapes=[
            pltpu.VMEM((rows, DEPTH), BF16),
            pltpu.VMEM((rows, DEPTH), BF16),
            pltpu.VMEM((DEPTH, width), BF16),
            pltpu.VMEM((ports.shape[0], width), BF16),
        ],
        compiler_params=pltpu.CompilerParams(vmem_limit_bytes=48 * 2**20),
        cost_estimate=pl.CostEstimate(
            flops=2 * pairs * (2 * DEPTH + LANES), bytes_accessed=2**21, transcendentals=pairs
        ),
        name="volts",
    )(targets, sources, ports)


def per_device(
    target_position,
    target_vector,
    target_radius,
    source_position,
    source_vector,
    source_radius,
    source_current,
    incidence,
    excitation,
):
    count = target_radius.shape[0]
    targets = jnp.concatenate(
        [target_position, target_radius[None], target_vector, jnp.zeros((1, count), F32)], 0
    )
    sources = jnp.concatenate(
        [
            source_position.reshape(-1),
            source_radius,
            source_vector.reshape(-1),
            source_current,
            incidence.astype(F32),
        ]
    ).reshape(-1, LANES)
    plane = SHAPE[0] * SHAPE[1]
    copies = jnp.broadcast_to(targets[None], (plane,) + targets.shape)
    row_targets = lax.all_to_all(copies, ("y", "x"), 0, 0, tiled=True)
    all_sources = lax.all_gather(sources, ("zh", "zl", "c"), axis=0, tiled=False)
    partial = volts(row_targets, all_sources, excitation.astype(F32)[:, None])
    shares = lax.all_to_all(
        partial.reshape(plane, count, partial.shape[1]), ("y", "x"), 0, 0, tiled=True
    )
    return jnp.sum(shares, 0)


def solution(mesh):
    fine = Mesh(mesh.devices.reshape(SHAPE), AXES)
    placed = (P(None, AXES), P(None, AXES), P(AXES), P(None, AXES), P(None, AXES))
    placed += (P(AXES), P(AXES), P(AXES), P())
    return jax.shard_map(
        per_device, mesh=fine, in_specs=placed, out_specs=P(AXES, None), check_vma=False
    )
```

```python
import jax
import jax.numpy as jnp
from jax import lax
from jax.experimental import pallas as pl
from jax.experimental.pallas import tpu as pltpu
from jax.sharding import Mesh, PartitionSpec as P

BF16 = jnp.bfloat16
F32 = jnp.float32
DEPTH = 64
LANES = 128
COUNT = 64
WIDTH = 1024
AXES = ("y", "x", "zh", "zl", "c")
SHAPE = (4, 4, 4, 2, 2)
SHIFTS = (0, 1, 3, 2)


def split3(x):
    high = x.astype(BF16).astype(F32)
    rest = x - high
    middle = rest.astype(BF16).astype(F32)
    low = (rest - middle).astype(BF16).astype(F32)
    return high, middle, low


def centred(x):
    row = lax.broadcasted_iota(jnp.int32, x.shape, 0)
    x = jnp.where(row < 3, x - 2.0, x)
    norm = jnp.sum(jnp.where(row < 4, x * x, 0.0), axis=0, keepdims=True)
    return row, x, split3(norm)


def source_features(x):
    row, x, (n_high, n_middle, n_low) = centred(x)
    high, middle, low = split3(x)
    norms = jnp.where(
        row == 0,
        n_high,
        jnp.where(row == 1, n_middle, jnp.where(row == 2, n_low, jnp.where(row < 6, 1.0, 0.0))),
    )
    parts = [high, high, high, middle, middle, low, norms, jnp.zeros_like(x)]
    return jnp.concatenate(parts, 0)


def target_features(x):
    row, x, (n_high, n_middle, n_low) = centred(x)
    high, middle, low = split3(x)
    norms = jnp.where(
        row < 3,
        1.0,
        jnp.where(row == 3, n_high, jnp.where(row == 4, n_middle, jnp.where(row == 5, n_low, 0.0))),
    )
    weight = jnp.where(row < 3, -2.0, jnp.where(row == 3, 2.0, 0.0))
    parts = [p * weight for p in (high, middle, low, high, middle, high)]
    return jnp.concatenate(parts + [norms, jnp.zeros_like(x)], 0)


def pack_kernel(t_pos, t_vec, t_rad, s_pos, s_vec, s_rad, s_cur, inc, exc, targets, copies, ports):
    count = t_rad.shape[1]
    one = jnp.concatenate([t_pos[...], t_rad[...], t_vec[...], jnp.zeros((1, count), F32)], 0)
    targets[...] = jnp.concatenate([one, jnp.zeros((8, LANES - count), F32)], 1)
    sources = copies.at[0]
    for r in range(8):
        here = slice(r * LANES, (r + 1) * LANES)
        for q in range(3):
            sources[8 * q + r : 8 * q + r + 1, :] = s_pos[q : q + 1, here]
            sources[8 * q + r + 32 : 8 * q + r + 33, :] = s_vec[q : q + 1, here]
    sources[24:32, :] = s_rad[...]
    sources[56:64, :] = s_cur[...]
    sources[64:72, :] = inc[...].astype(F32)
    for i in range(1, copies.shape[0]):
        copies[i] = copies[0]
    ports[...] = jnp.transpose(jnp.broadcast_to(exc[...].astype(F32), ports.shape))


def pack(plane, *arrays):
    vmem = pl.BlockSpec(memory_space=pltpu.VMEM)
    return pl.pallas_call(
        pack_kernel,
        out_shape=[
            jax.ShapeDtypeStruct((8, LANES), F32),
            jax.ShapeDtypeStruct((plane, 72, LANES), F32),
            jax.ShapeDtypeStruct((LANES, LANES), F32),
        ],
        in_specs=[vmem] * len(arrays),
        out_specs=[vmem] * 3,
        name="pack",
    )(*arrays)


def prepare_targets(same, other, squared, vectors):
    for j in range(2 * len(SHIFTS)):
        here = slice(j * COUNT, (j + 1) * COUNT)
        x = (same, other)[j // len(SHIFTS)][j % len(SHIFTS)]
        squared[here, :] = jnp.transpose(target_features(x))[:COUNT].astype(BF16)
        for d in range(3):
            spread = jnp.broadcast_to(x[4 + d : 5 + d, :], (LANES, LANES))
            vectors[d, here, :] = jnp.transpose(spread)[:COUNT]


def add_sources(sources, ports, squared, vectors, total, even, odd):
    port = ports[...]
    blocks = sources.shape[0]

    def prepare(b, features, raw, currents):
        for r in range(WIDTH // LANES):
            here = slice(r * LANES, (r + 1) * LANES)
            x = sources[b, pl.ds(r, 8, stride=8), :]
            features[:, here] = source_features(x).astype(BF16)
            raw[:, here] = x
            current = sources[b, pl.ds(56 + r, 1), :]
            incidence = sources[b, pl.ds(64 + r, 1), :]
            currents[:, here] = jnp.where(port == incidence, current, 0.0).astype(BF16)

    def add(features, raw, currents):
        step = 256
        for s in range(0, WIDTH, step):
            these = slice(s, s + step)
            distance = jnp.dot(squared[...], features[:, these], preferred_element_type=F32)
            alignment = []
            for t in range(s, s + step, LANES):
                here = slice(t, t + LANES)
                alignment.append(
                    vectors[0] * raw[4:5, here]
                    + vectors[1] * raw[5:6, here]
                    + vectors[2] * raw[6:7, here]
                )
            inductance = jnp.concatenate(alignment, 1) * lax.rsqrt(distance)
            total[...] += lax.dot_general(
                inductance.astype(BF16),
                currents[:, these],
                (((1,), (1,)), ((), ())),
                preferred_element_type=F32,
            )

    prepare(0, *even)

    def two(i, carry):
        prepare(2 * i + 1, *odd)
        add(*even)
        prepare(jnp.minimum(2 * i + 2, blocks - 1), *even)
        add(*odd)
        return carry

    lax.fori_loop(0, blocks // 2, two, 0)


def near_kernel(same, other, sources, ports, squared, vectors, total, *buffers):
    prepare_targets(same, other, squared, vectors)
    total[...] = jnp.zeros_like(total)
    add_sources(sources, ports, squared, vectors, total, buffers[:3], buffers[3:])


def far_kernel(mine, sources, ports, squared, vectors, start, keep, send, total, *buffers):
    total[...] = start[...]
    add_sources(sources, ports, squared, vectors, total, buffers[:3], buffers[3:])
    half = total.shape[0] // 2
    for j, shift in enumerate(SHIFTS):
        zh = lax.rem(mine[0] + SHAPE[2] - shift, SHAPE[2])
        keep[zh] = total[j * COUNT : (j + 1) * COUNT, :]
        send[zh] = total[half + j * COUNT : half + (j + 1) * COUNT, :]


ROWS = 2 * len(SHIFTS) * COUNT
BUFFERS = [
    pltpu.VMEM((DEPTH, WIDTH), BF16),
    pltpu.VMEM((8, WIDTH), F32),
    pltpu.VMEM((LANES, WIDTH), BF16),
] * 2


def options(sources):
    pairs = ROWS * sources.shape[0] * WIDTH
    return {
        "compiler_params": pltpu.CompilerParams(vmem_limit_bytes=24 * 2**20),
        "cost_estimate": pl.CostEstimate(
            flops=2 * pairs * (DEPTH + LANES), bytes_accessed=2**21, transcendentals=pairs
        ),
    }


def near_volts(same, other, sources, ports):
    vmem = pl.BlockSpec(memory_space=pltpu.VMEM)
    return pl.pallas_call(
        near_kernel,
        out_shape=[
            jax.ShapeDtypeStruct((ROWS, DEPTH), BF16),
            jax.ShapeDtypeStruct((3, ROWS, LANES), F32),
            jax.ShapeDtypeStruct((ROWS, LANES), F32),
        ],
        in_specs=[vmem] * 4,
        out_specs=[vmem] * 3,
        scratch_shapes=BUFFERS,
        name="near_volts",
        **options(sources),
    )(same, other, sources, ports)


def far_volts(mine, sources, ports, squared, vectors, start):
    vmem = pl.BlockSpec(memory_space=pltpu.VMEM)
    return pl.pallas_call(
        far_kernel,
        out_shape=[jax.ShapeDtypeStruct((len(SHIFTS), COUNT, LANES), F32)] * 2,
        in_specs=[pl.BlockSpec(memory_space=pltpu.SMEM)] + [vmem] * 5,
        out_specs=[vmem] * 2,
        scratch_shapes=[pltpu.VMEM((ROWS, LANES), F32)] + BUFFERS,
        name="far_volts",
        **options(sources),
    )(mine, sources, ports, squared, vectors, start)


def per_device(
    target_position,
    target_vector,
    target_radius,
    source_position,
    source_vector,
    source_radius,
    source_current,
    incidence,
    excitation,
):
    plane = SHAPE[0] * SHAPE[1]
    block, copies, ports = pack(
        plane,
        target_position,
        target_vector,
        target_radius[None],
        source_position,
        source_vector,
        source_radius.reshape(8, LANES),
        source_current.reshape(8, LANES),
        incidence.reshape(8, LANES),
        excitation[None],
    )
    sources = lax.all_to_all(copies, ("y", "x"), 0, 0, tiled=True)
    zh = SHAPE[2]
    same = [block] + [
        lax.ppermute(block, "zh", [(i, (i + k) % zh) for i in range(zh)]) for k in SHIFTS[1:]
    ]
    same = jnp.stack(same)
    swap = [(0, 1), (1, 0)]
    other = lax.ppermute(same, "c", swap)
    mine = lax.axis_index("zh").astype(jnp.int32)[None]
    sources, same, other = lax.optimization_barrier((sources, same, other))
    far = lax.ppermute(sources, "zl", swap)
    prepared = near_volts(same, other, sources, ports)
    keep, send = far_volts(mine, far, ports, *prepared)
    partial = keep + lax.ppermute(send, "c", swap)
    return jnp.sum(lax.all_to_all(partial, "zh", 0, 0, tiled=True), 0)


def solution(mesh):
    fine = Mesh(mesh.devices.reshape(SHAPE), AXES)
    placed = (P(None, AXES), P(None, AXES), P(AXES), P(None, AXES), P(None, AXES))
    placed += (P(AXES), P(AXES), P(AXES), P())
    return jax.shard_map(
        per_device, mesh=fine, in_specs=placed, out_specs=P(AXES, None), check_vma=False
    )
```

```python
import jax
import jax.numpy as jnp
from jax import lax
from jax.experimental import pallas as pl
from jax.experimental.pallas import tpu as pltpu
from jax.sharding import Mesh, PartitionSpec as P

BF16 = jnp.bfloat16
F32 = jnp.float32
DEPTH = 64
LANES = 128
COUNT = 64
WIDTH = 1024
AXES = ("y", "x", "zh", "zl", "c")
SHAPE = (4, 4, 4, 2, 2)
FLIPS = (0, 1, 2, 3)


def split3(x):
    high = x.astype(BF16).astype(F32)
    rest = x - high
    middle = rest.astype(BF16).astype(F32)
    low = (rest - middle).astype(BF16).astype(F32)
    return high, middle, low


def centred(x):
    row = lax.broadcasted_iota(jnp.int32, x.shape, 0)
    x = jnp.where(row < 3, x - 2.0, x)
    norm = jnp.sum(jnp.where(row < 4, x * x, 0.0), axis=0, keepdims=True)
    return row, x, split3(norm)


def source_features(x):
    row, x, (n_high, n_middle, n_low) = centred(x)
    high, middle, low = split3(x)
    norms = jnp.where(
        row == 0,
        n_high,
        jnp.where(row == 1, n_middle, jnp.where(row == 2, n_low, jnp.where(row < 6, 1.0, 0.0))),
    )
    parts = [high, high, high, middle, middle, low, norms, jnp.zeros_like(x)]
    return jnp.concatenate(parts, 0)


def target_features(x):
    row, x, (n_high, n_middle, n_low) = centred(x)
    high, middle, low = split3(x)
    norms = jnp.where(
        row < 3,
        1.0,
        jnp.where(row == 3, n_high, jnp.where(row == 4, n_middle, jnp.where(row == 5, n_low, 0.0))),
    )
    weight = jnp.where(row < 3, -2.0, jnp.where(row == 3, 2.0, 0.0))
    parts = [p * weight for p in (high, middle, low, high, middle, high)]
    return jnp.concatenate(parts + [norms, jnp.zeros_like(x)], 0)


def pack_targets_kernel(position, vector, radius, block):
    count = radius.shape[1]
    rows = [position[...], radius[...], vector[...], jnp.zeros((1, count), F32)]
    wide = [jnp.concatenate(rows, 0), jnp.zeros((8, LANES - count), F32)]
    block[...] = jnp.concatenate(wide, 1)


def pack_sources_kernel(position, vector, radius, current, incidence, excitation, copies, ports):
    sources = copies.at[0]
    for r in range(8):
        here = slice(r * LANES, (r + 1) * LANES)
        for q in range(3):
            sources[8 * q + r : 8 * q + r + 1, :] = position[q : q + 1, here]
            sources[8 * q + r + 32 : 8 * q + r + 33, :] = vector[q : q + 1, here]
    sources[24:32, :] = radius[...]
    sources[56:64, :] = current[...]
    sources[64:72, :] = incidence[...].astype(F32)
    for i in range(1, copies.shape[0]):
        copies[i] = copies[0]
    ports[...] = jnp.transpose(jnp.broadcast_to(excitation[...].astype(F32), ports.shape))


def pack(kernel, name, shapes, *arrays):
    vmem = pl.BlockSpec(memory_space=pltpu.VMEM)
    return pl.pallas_call(
        kernel,
        out_shape=[jax.ShapeDtypeStruct(shape, F32) for shape in shapes],
        in_specs=[vmem] * len(arrays),
        out_specs=[vmem] * len(shapes),
        name=name,
    )(*arrays)


def prepare_targets(pairs, squared, vectors):
    for j in range(2 * len(FLIPS)):
        here = slice(j * COUNT, (j + 1) * COUNT)
        x = pairs[j % len(FLIPS)][j // len(FLIPS)]
        squared[here, :] = jnp.transpose(target_features(x))[:COUNT].astype(BF16)
        for d in range(3):
            spread = jnp.broadcast_to(x[4 + d : 5 + d, :], (LANES, LANES))
            vectors[d, here, :] = jnp.transpose(spread)[:COUNT]


def add_sources(sources, ports, squared, vectors, total, even, odd):
    port = ports[...]
    blocks = sources.shape[0]

    def prepare(b, features, raw, currents):
        for r in range(WIDTH // LANES):
            here = slice(r * LANES, (r + 1) * LANES)
            x = sources[b, pl.ds(r, 8, stride=8), :]
            features[:, here] = source_features(x).astype(BF16)
            raw[:, here] = x
            current = sources[b, pl.ds(56 + r, 1), :]
            incidence = sources[b, pl.ds(64 + r, 1), :]
            matched = jnp.where(port == incidence, current, 0.0)
            currents[here, :] = jnp.transpose(matched).astype(BF16)

    def add(features, raw, currents):
        step = 256
        for s in range(0, WIDTH, step):
            these = slice(s, s + step)
            distance = jnp.dot(squared[...], features[:, these], preferred_element_type=F32)
            alignment = []
            for t in range(s, s + step, LANES):
                here = slice(t, t + LANES)
                alignment.append(
                    vectors[0] * raw[4:5, here]
                    + vectors[1] * raw[5:6, here]
                    + vectors[2] * raw[6:7, here]
                )
            inductance = jnp.concatenate(alignment, 1) * lax.rsqrt(distance)
            total[...] += jnp.dot(
                inductance.astype(BF16), currents[these, :], preferred_element_type=F32
            )

    prepare(0, *even)

    def two(i, carry):
        prepare(2 * i + 1, *odd)
        add(*even)
        prepare(jnp.minimum(2 * i + 2, blocks - 1), *even)
        add(*odd)
        return carry

    lax.fori_loop(0, blocks // 2, two, 0)


def near_kernel(*refs):
    pairs, refs = refs[: len(FLIPS)], refs[len(FLIPS) :]
    sources, ports, squared, vectors, total, *buffers = refs
    prepare_targets(pairs, squared, vectors)
    total[...] = jnp.zeros_like(total)
    add_sources(sources, ports, squared, vectors, total, buffers[:3], buffers[3:])


def far_kernel(sources, ports, squared, vectors, start, keep, send, total, *buffers):
    total[...] = start[...]
    add_sources(sources, ports, squared, vectors, total, buffers[:3], buffers[3:])
    half = total.shape[0] // 2
    keep[...] = total[:half, :]
    send[...] = total[half:, :]


ROWS = 2 * len(FLIPS) * COUNT
BUFFERS = [
    pltpu.VMEM((DEPTH, WIDTH), BF16),
    pltpu.VMEM((8, WIDTH), F32),
    pltpu.VMEM((WIDTH, LANES), BF16),
] * 2


def options(sources):
    pairs = ROWS * sources.shape[0] * WIDTH
    return {
        "compiler_params": pltpu.CompilerParams(vmem_limit_bytes=24 * 2**20),
        "cost_estimate": pl.CostEstimate(
            flops=2 * pairs * (DEPTH + LANES), bytes_accessed=2**21, transcendentals=pairs
        ),
    }


def near_volts(pairs, sources, ports):
    vmem = pl.BlockSpec(memory_space=pltpu.VMEM)
    return pl.pallas_call(
        near_kernel,
        out_shape=[
            jax.ShapeDtypeStruct((ROWS, DEPTH), BF16),
            jax.ShapeDtypeStruct((3, ROWS, LANES), F32),
            jax.ShapeDtypeStruct((ROWS, LANES), F32),
        ],
        in_specs=[vmem] * (len(FLIPS) + 2),
        out_specs=[vmem] * 3,
        scratch_shapes=BUFFERS,
        name="near_volts",
        **options(sources),
    )(*pairs, sources, ports)


def far_volts(sources, ports, squared, vectors, start):
    vmem = pl.BlockSpec(memory_space=pltpu.VMEM)
    return pl.pallas_call(
        far_kernel,
        out_shape=[jax.ShapeDtypeStruct((ROWS // 2, LANES), F32)] * 2,
        in_specs=[vmem] * 5,
        out_specs=[vmem] * 2,
        scratch_shapes=[pltpu.VMEM((ROWS, LANES), F32)] + BUFFERS,
        name="far_volts",
        **options(sources),
    )(sources, ports, squared, vectors, start)


def per_device(
    target_position,
    target_vector,
    target_radius,
    source_position,
    source_vector,
    source_radius,
    source_current,
    incidence,
    excitation,
):
    plane = SHAPE[0] * SHAPE[1]
    (block,) = pack(
        pack_targets_kernel,
        "pack_targets",
        [(8, LANES)],
        target_position,
        target_vector,
        target_radius[None],
    )
    swap = [(0, 1), (1, 0)]
    other = lax.ppermute(block, "c", swap)
    copies, ports = pack(
        pack_sources_kernel,
        "pack_sources",
        [(plane, 72, LANES), (LANES, LANES)],
        source_position,
        source_vector,
        source_radius.reshape(8, LANES),
        source_current.reshape(8, LANES),
        incidence.reshape(8, LANES),
        excitation[None],
    )
    copies, other = lax.optimization_barrier((copies, other))
    sources = lax.all_to_all(copies, ("y", "x"), 0, 0, tiled=True)
    pair = jnp.stack([block, other])
    zh = range(SHAPE[2])
    pairs = [pair] + [lax.ppermute(pair, "zh", [(i, i ^ k) for i in zh]) for k in FLIPS[1:]]
    sources, pairs = lax.optimization_barrier((sources, pairs))
    far = lax.ppermute(sources, "zl", swap)
    prepared = near_volts(pairs, sources, ports)
    keep, send = far_volts(far, ports, *prepared)
    partial = (keep + lax.ppermute(send, "c", swap)).reshape(len(FLIPS), COUNT, LANES)
    shares = [partial[0]]
    shares += [lax.ppermute(partial[k], "zh", [(i, i ^ k) for i in zh]) for k in FLIPS[1:]]
    return sum(shares[1:], shares[0])


def solution(mesh):
    fine = Mesh(mesh.devices.reshape(SHAPE), AXES)
    placed = (P(None, AXES), P(None, AXES), P(AXES), P(None, AXES), P(None, AXES))
    placed += (P(AXES), P(AXES), P(AXES), P())
    return jax.shard_map(
        per_device, mesh=fine, in_specs=placed, out_specs=P(AXES, None), check_vma=False
    )
```

```python
import jax
import jax.numpy as jnp
from jax import lax
from jax.experimental import pallas as pl
from jax.experimental.pallas import tpu as pltpu
from jax.sharding import Mesh, PartitionSpec as P

BF16 = jnp.bfloat16
F32 = jnp.float32
DEPTH = 64
LANES = 128
COUNT = 64
WIDTH = 1024
AXES = ("y", "x", "zh", "zl", "c")
SHAPE = (4, 4, 4, 2, 2)
FLIPS = (0, 2, 1, 3)


def split3(x):
    high = x.astype(BF16).astype(F32)
    rest = x - high
    middle = rest.astype(BF16).astype(F32)
    low = (rest - middle).astype(BF16).astype(F32)
    return high, middle, low


def centred(x):
    row = lax.broadcasted_iota(jnp.int32, x.shape, 0)
    x = jnp.where(row < 3, x - 2.0, x)
    norm = jnp.sum(jnp.where(row < 4, x * x, 0.0), axis=0, keepdims=True)
    return row, x, split3(norm)


def source_features(x):
    row, x, (n_high, n_middle, n_low) = centred(x)
    high, middle, low = split3(x)
    norms = jnp.where(
        row == 0,
        n_high,
        jnp.where(row == 1, n_middle, jnp.where(row == 2, n_low, jnp.where(row < 6, 1.0, 0.0))),
    )
    parts = [high, high, high, middle, middle, low, norms, jnp.zeros_like(x)]
    return jnp.concatenate(parts, 0)


def target_features(x):
    row, x, (n_high, n_middle, n_low) = centred(x)
    high, middle, low = split3(x)
    norms = jnp.where(
        row < 3,
        1.0,
        jnp.where(row == 3, n_high, jnp.where(row == 4, n_middle, jnp.where(row == 5, n_low, 0.0))),
    )
    weight = jnp.where(row < 3, -2.0, jnp.where(row == 3, 2.0, 0.0))
    parts = [p * weight for p in (high, middle, low, high, middle, high)]
    return jnp.concatenate(parts + [norms, jnp.zeros_like(x)], 0)


def pack_kernel(t_position, t_vector, t_radius, *refs):
    position, vector, radius, current, incidence, excitation, block, copies, ports = refs
    count = t_radius.shape[1]
    rows = [t_position[...], t_radius[...], t_vector[...], jnp.zeros((1, count), F32)]
    wide = [jnp.concatenate(rows, 0), jnp.zeros((8, LANES - count), F32)]
    block[...] = jnp.concatenate(wide, 1)
    sources = copies.at[0]
    for r in range(8):
        here = slice(r * LANES, (r + 1) * LANES)
        for q in range(3):
            sources[8 * q + r : 8 * q + r + 1, :] = position[q : q + 1, here]
            sources[8 * q + r + 32 : 8 * q + r + 33, :] = vector[q : q + 1, here]
    sources[24:32, :] = radius[...]
    sources[56:64, :] = current[...]
    sources[64:72, :] = incidence[...].astype(F32)
    for i in range(1, copies.shape[0]):
        copies[i] = copies[0]
    ports[...] = jnp.transpose(jnp.broadcast_to(excitation[...].astype(F32), ports.shape))


def pack(shapes, *arrays):
    vmem = pl.BlockSpec(memory_space=pltpu.VMEM)
    return pl.pallas_call(
        pack_kernel,
        out_shape=[jax.ShapeDtypeStruct(shape, F32) for shape in shapes],
        in_specs=[vmem] * len(arrays),
        out_specs=[vmem] * len(shapes),
        name="pack",
    )(*arrays)


def prepare_targets(pairs, squared, vectors):
    for j in range(2 * len(FLIPS)):
        here = slice(j * COUNT, (j + 1) * COUNT)
        x = pairs[j % len(FLIPS)][j // len(FLIPS)]
        squared[here, :] = jnp.transpose(target_features(x))[:COUNT].astype(BF16)
        for d in range(3):
            spread = jnp.broadcast_to(x[4 + d : 5 + d, :], (LANES, LANES))
            vectors[d, here, :] = jnp.transpose(spread)[:COUNT]


def add_sources(sources, ports, squared, vectors, total, even, odd):
    port = ports[...]
    blocks = sources.shape[0]

    def prepare(b, features, raw, currents):
        for r in range(WIDTH // LANES):
            here = slice(r * LANES, (r + 1) * LANES)
            x = sources[b, pl.ds(r, 8, stride=8), :]
            features[:, here] = source_features(x).astype(BF16)
            raw[:, here] = x
            current = sources[b, pl.ds(56 + r, 1), :]
            incidence = sources[b, pl.ds(64 + r, 1), :]
            matched = jnp.where(port == incidence, current, 0.0)
            currents[here, :] = jnp.transpose(matched).astype(BF16)

    def add(features, raw, currents):
        step = 256
        for s in range(0, WIDTH, step):
            these = slice(s, s + step)
            distance = jnp.dot(squared[...], features[:, these], preferred_element_type=F32)
            alignment = []
            for t in range(s, s + step, LANES):
                here = slice(t, t + LANES)
                alignment.append(
                    vectors[0] * raw[4:5, here]
                    + vectors[1] * raw[5:6, here]
                    + vectors[2] * raw[6:7, here]
                )
            inductance = jnp.concatenate(alignment, 1) * lax.rsqrt(distance)
            total[...] += jnp.dot(
                inductance.astype(BF16), currents[these, :], preferred_element_type=F32
            )

    prepare(0, *even)

    def two(i, carry):
        prepare(2 * i + 1, *odd)
        add(*even)
        prepare(jnp.minimum(2 * i + 2, blocks - 1), *even)
        add(*odd)
        return carry

    lax.fori_loop(0, blocks // 2, two, 0)


def near_kernel(*refs):
    pairs, refs = refs[: len(FLIPS)], refs[len(FLIPS) :]
    sources, ports, squared, vectors, total, *buffers = refs
    prepare_targets(pairs, squared, vectors)
    total[...] = jnp.zeros_like(total)
    add_sources(sources, ports, squared, vectors, total, buffers[:3], buffers[3:])


def far_kernel(sources, ports, squared, vectors, start, keep, send, total, *buffers):
    total[...] = start[...]
    add_sources(sources, ports, squared, vectors, total, buffers[:3], buffers[3:])
    half = total.shape[0] // 2
    keep[...] = total[:half, :]
    send[...] = total[half:, :]


ROWS = 2 * len(FLIPS) * COUNT
BUFFERS = [
    pltpu.VMEM((DEPTH, WIDTH), BF16),
    pltpu.VMEM((8, WIDTH), F32),
    pltpu.VMEM((WIDTH, LANES), BF16),
] * 2


def options(sources):
    pairs = ROWS * sources.shape[0] * WIDTH
    return {
        "compiler_params": pltpu.CompilerParams(vmem_limit_bytes=24 * 2**20),
        "cost_estimate": pl.CostEstimate(
            flops=2 * pairs * (DEPTH + LANES), bytes_accessed=2**21, transcendentals=pairs
        ),
    }


def near_volts(pairs, sources, ports):
    vmem = pl.BlockSpec(memory_space=pltpu.VMEM)
    return pl.pallas_call(
        near_kernel,
        out_shape=[
            jax.ShapeDtypeStruct((ROWS, DEPTH), BF16),
            jax.ShapeDtypeStruct((3, ROWS, LANES), F32),
            jax.ShapeDtypeStruct((ROWS, LANES), F32),
        ],
        in_specs=[vmem] * (len(FLIPS) + 2),
        out_specs=[vmem] * 3,
        scratch_shapes=BUFFERS,
        name="near_volts",
        **options(sources),
    )(*pairs, sources, ports)


def far_volts(sources, ports, squared, vectors, start):
    vmem = pl.BlockSpec(memory_space=pltpu.VMEM)
    return pl.pallas_call(
        far_kernel,
        out_shape=[jax.ShapeDtypeStruct((ROWS // 2, LANES), F32)] * 2,
        in_specs=[vmem] * 5,
        out_specs=[vmem] * 2,
        scratch_shapes=[pltpu.VMEM((ROWS, LANES), F32)] + BUFFERS,
        name="far_volts",
        **options(sources),
    )(sources, ports, squared, vectors, start)


def per_device(
    target_position,
    target_vector,
    target_radius,
    source_position,
    source_vector,
    source_radius,
    source_current,
    incidence,
    excitation,
):
    plane = SHAPE[0] * SHAPE[1]
    block, copies, ports = pack(
        [(8, LANES), (plane, 72, LANES), (LANES, LANES)],
        target_position,
        target_vector,
        target_radius[None],
        source_position,
        source_vector,
        source_radius.reshape(8, LANES),
        source_current.reshape(8, LANES),
        incidence.reshape(8, LANES),
        excitation[None],
    )
    swap = [(0, 1), (1, 0)]
    other = lax.ppermute(block, "c", swap)
    sources = lax.all_to_all(copies, ("y", "x"), 0, 0, tiled=True)
    pair = jnp.stack([block, other])
    zh = range(SHAPE[2])
    pairs = [pair] + [lax.ppermute(pair, "zh", [(i, i ^ k) for i in zh]) for k in FLIPS[1:]]
    sources, pairs = lax.optimization_barrier((sources, pairs))
    far = lax.ppermute(sources, "zl", swap)
    prepared = near_volts(pairs, sources, ports)
    keep, send = far_volts(far, ports, *prepared)
    partial = (keep + lax.ppermute(send, "c", swap)).reshape(len(FLIPS), COUNT, LANES)
    shares = [partial[0]]
    for j, k in enumerate(FLIPS[1:], 1):
        shares.append(lax.ppermute(partial[j], "zh", [(i, i ^ k) for i in zh]))
    return sum(shares[1:], shares[0])


def solution(mesh):
    fine = Mesh(mesh.devices.reshape(SHAPE), AXES)
    placed = (P(None, AXES), P(None, AXES), P(AXES), P(None, AXES), P(None, AXES))
    placed += (P(AXES), P(AXES), P(AXES), P())
    return jax.shard_map(
        per_device, mesh=fine, in_specs=placed, out_specs=P(AXES, None), check_vma=False
    )
```

```python
import jax
import jax.numpy as jnp
from jax import lax
from jax.experimental import pallas as pl
from jax.experimental.pallas import tpu as pltpu
from jax.sharding import Mesh, PartitionSpec as P

BF16 = jnp.bfloat16
F32 = jnp.float32
TILE = 256
UNROLL = 8
DEPTH = 32
LANES = 128
MIDDLE = 2.0
COUNT = 64
WIDTH = 1024
AXES = ("y", "x", "zh", "zl", "c")
SHAPE = (4, 4, 4, 2, 2)
FLIPS = (0, 2, 1, 3)


def split3(x):
    high = x.astype(BF16).astype(F32)
    rest = x - high
    middle = rest.astype(BF16).astype(F32)
    low = (rest - middle).astype(BF16).astype(F32)
    return high, middle, low


def doubled(x):
    row = lax.broadcasted_iota(jnp.int32, x.shape, 0)
    x = jnp.concatenate([x[:4], x[:4]], 0)
    norm = jnp.sum((x * x)[:4], axis=0, keepdims=True)
    return row, split3(x), split3(norm)


def by_half(row, low, high):
    return jnp.where(row < 4, low, high)


def by_row(row, values, rest):
    for i, value in reversed(list(enumerate(values))):
        rest = jnp.where(row == i, value, rest)
    return rest


def source_features(x):
    row, (high, middle, low), norm = doubled(x)
    ones = jnp.where(row < 6, 1.0, 0.0)
    groups = [high, by_half(row, high, middle), by_half(row, middle, low), by_row(row, norm, ones)]
    return jnp.concatenate(groups, 0)


def target_features(x):
    row, (high, middle, low), norm = doubled(x)
    weight = jnp.where((row & 3) < 3, -2.0, 2.0)
    groups = [by_half(row, high, middle), by_half(row, low, high), by_half(row, middle, high)]
    last = by_row(row, (1.0, 1.0, 1.0) + norm, 0.0)
    return jnp.concatenate([g * weight for g in groups] + [last], 0)


def pack_kernel(t_position, t_vector, t_radius, *refs):
    position, vector, radius, current, incidence, excitation, block, copies, ports = refs
    count = t_radius.shape[1]
    rows = [t_position[...] - MIDDLE, t_radius[...], t_vector[...], jnp.zeros((1, count), F32)]
    wide = [jnp.concatenate(rows, 0), jnp.zeros((8, LANES - count), F32)]
    block[...] = jnp.concatenate(wide, 1)
    sources = copies.at[0]
    for r in range(8):
        here = slice(r * LANES, (r + 1) * LANES)
        for q in range(3):
            sources[8 * q + r : 8 * q + r + 1, :] = position[q : q + 1, here] - MIDDLE
            sources[8 * q + r + 32 : 8 * q + r + 33, :] = vector[q : q + 1, here]
    sources[24:32, :] = radius[...]
    sources[56:64, :] = current[...]
    sources[64:72, :] = incidence[...].astype(F32)
    for i in range(1, copies.shape[0]):
        copies[i] = copies[0]
    ports[...] = jnp.transpose(jnp.broadcast_to(excitation[...].astype(F32), ports.shape))


def pack(shapes, *arrays):
    vmem = pl.BlockSpec(memory_space=pltpu.VMEM)
    return pl.pallas_call(
        pack_kernel,
        out_shape=[jax.ShapeDtypeStruct(shape, F32) for shape in shapes],
        in_specs=[vmem] * len(arrays),
        out_specs=[vmem] * len(shapes),
        name="pack",
    )(*arrays)


def prepare_targets(pairs, squared, vectors):
    for j in range(2 * len(FLIPS)):
        here = slice(j * COUNT, (j + 1) * COUNT)
        x = pairs[j % len(FLIPS)][j // len(FLIPS)]
        squared[here, :] = jnp.transpose(target_features(x))[:COUNT].astype(BF16)
        for d in range(3):
            spread = jnp.broadcast_to(x[4 + d : 5 + d, :], (LANES, LANES))
            vectors[d, here, :] = jnp.transpose(spread)[:COUNT]


def add_sources(sources, ports, squared, vectors, total, even, odd):
    port = ports[...]
    blocks = sources.shape[0]

    def prepare(b, features, currents):
        for r in range(WIDTH // LANES):
            here = slice(r * LANES, (r + 1) * LANES)
            x = sources[b, pl.ds(r, 8, stride=8), :]
            features[:, here] = source_features(x).astype(BF16)
            current = sources[b, pl.ds(56 + r, 1), :]
            incidence = sources[b, pl.ds(64 + r, 1), :]
            matched = jnp.where(port == incidence, current, 0.0)
            currents[here, :] = jnp.transpose(matched).astype(BF16)

    def inductance(b, k, features):
        these = slice(k * TILE, (k + 1) * TILE)
        distance = jnp.dot(squared[...], features[:, these], preferred_element_type=F32)
        alignment = []
        for r in range(k * TILE // LANES, (k + 1) * TILE // LANES):
            x, y, z = (sources[b, pl.ds(8 * d + r, 1), :] for d in (4, 5, 6))
            alignment.append(vectors[0] * x + vectors[1] * y + vectors[2] * z)
        return (jnp.concatenate(alignment, 1) * lax.rsqrt(distance)).astype(BF16)

    def add(b, features, currents):
        for k in range(WIDTH // TILE):
            these = slice(k * TILE, (k + 1) * TILE)
            total[...] += jnp.dot(
                inductance(b, k, features), currents[these, :], preferred_element_type=F32
            )

    prepare(0, *even)

    def some(i, carry):
        for j in range(UNROLL):
            b = UNROLL * i + j
            this, other = (even, odd) if j % 2 == 0 else (odd, even)
            prepare(jnp.minimum(b + 1, blocks - 1), *other)
            add(b, *this)
        return carry

    lax.fori_loop(0, blocks // UNROLL, some, 0)


def near_kernel(*refs):
    pairs, refs = refs[: len(FLIPS)], refs[len(FLIPS) :]
    sources, ports, squared, vectors, total, *buffers = refs
    prepare_targets(pairs, squared, vectors)
    total[...] = jnp.zeros_like(total)
    add_sources(sources, ports, squared, vectors, total, buffers[:2], buffers[2:])


def far_kernel(sources, ports, squared, vectors, start, keep, send, total, *buffers):
    total[...] = start[...]
    add_sources(sources, ports, squared, vectors, total, buffers[:2], buffers[2:])
    half = total.shape[0] // 2
    keep[...] = total[:half, :]
    send[...] = total[half:, :]


ROWS = 2 * len(FLIPS) * COUNT
BUFFERS = [pltpu.VMEM((DEPTH, WIDTH), BF16), pltpu.VMEM((WIDTH, LANES), BF16)] * 2


def options(sources):
    pairs = ROWS * sources.shape[0] * WIDTH
    return {
        "compiler_params": pltpu.CompilerParams(vmem_limit_bytes=24 * 2**20),
        "cost_estimate": pl.CostEstimate(
            flops=2 * pairs * (DEPTH + LANES), bytes_accessed=2**21, transcendentals=pairs
        ),
    }


def near_volts(pairs, sources, ports):
    vmem = pl.BlockSpec(memory_space=pltpu.VMEM)
    return pl.pallas_call(
        near_kernel,
        out_shape=[
            jax.ShapeDtypeStruct((ROWS, DEPTH), BF16),
            jax.ShapeDtypeStruct((3, ROWS, LANES), F32),
            jax.ShapeDtypeStruct((ROWS, LANES), F32),
        ],
        in_specs=[vmem] * (len(FLIPS) + 2),
        out_specs=[vmem] * 3,
        scratch_shapes=BUFFERS,
        name="near_volts",
        **options(sources),
    )(*pairs, sources, ports)


def far_volts(sources, ports, squared, vectors, start):
    vmem = pl.BlockSpec(memory_space=pltpu.VMEM)
    return pl.pallas_call(
        far_kernel,
        out_shape=[jax.ShapeDtypeStruct((ROWS // 2, LANES), F32)] * 2,
        in_specs=[vmem] * 5,
        out_specs=[vmem] * 2,
        scratch_shapes=[pltpu.VMEM((ROWS, LANES), F32)] + BUFFERS,
        name="far_volts",
        **options(sources),
    )(sources, ports, squared, vectors, start)


def per_device(
    target_position,
    target_vector,
    target_radius,
    source_position,
    source_vector,
    source_radius,
    source_current,
    incidence,
    excitation,
):
    plane = SHAPE[0] * SHAPE[1]
    block, copies, ports = pack(
        [(8, LANES), (plane, 72, LANES), (LANES, LANES)],
        target_position,
        target_vector,
        target_radius[None],
        source_position,
        source_vector,
        source_radius.reshape(8, LANES),
        source_current.reshape(8, LANES),
        incidence.reshape(8, LANES),
        excitation[None],
    )
    swap = [(0, 1), (1, 0)]
    other = lax.ppermute(block, "c", swap)
    sources = lax.all_to_all(copies, ("y", "x"), 0, 0, tiled=True)
    pair = jnp.stack([block, other])
    zh = range(SHAPE[2])
    pairs = [pair] + [lax.ppermute(pair, "zh", [(i, i ^ k) for i in zh]) for k in FLIPS[1:]]
    sources, pairs = lax.optimization_barrier((sources, pairs))
    far = lax.ppermute(sources, "zl", swap)
    prepared = near_volts(pairs, sources, ports)
    keep, send = far_volts(far, ports, *prepared)
    partial = (keep + lax.ppermute(send, "c", swap)).reshape(len(FLIPS), COUNT, LANES)
    shares = [partial[0]]
    for j, k in enumerate(FLIPS[1:], 1):
        shares.append(lax.ppermute(partial[j], "zh", [(i, i ^ k) for i in zh]))
    return sum(shares[1:], shares[0])


def solution(mesh):
    fine = Mesh(mesh.devices.reshape(SHAPE), AXES)
    placed = (P(None, AXES), P(None, AXES), P(AXES), P(None, AXES), P(None, AXES))
    placed += (P(AXES), P(AXES), P(AXES), P())
    return jax.shard_map(
        per_device, mesh=fine, in_specs=placed, out_specs=P(AXES, None), check_vma=False
    )
```

```python
import jax
import jax.numpy as jnp
from jax import lax
from jax.experimental import pallas as pl
from jax.experimental.pallas import tpu as pltpu
from jax.sharding import Mesh, PartitionSpec as P

BF16 = jnp.bfloat16
F32 = jnp.float32
TILE = 256
UNROLL = 16
DEPTH = 32
LANES = 128
MIDDLE = 2.0
COUNT = 64
WIDTH = 1024
AXES = ("y", "x", "zh", "zl", "c")
SHAPE = (4, 4, 4, 2, 2)
FLIPS = (0, 2, 1, 3)


def split3(x):
    high = x.astype(BF16).astype(F32)
    rest = x - high
    middle = rest.astype(BF16).astype(F32)
    low = (rest - middle).astype(BF16).astype(F32)
    return high, middle, low


def doubled(x):
    row = lax.broadcasted_iota(jnp.int32, x.shape, 0)
    x = jnp.concatenate([x[:4], x[:4]], 0)
    norm = jnp.sum((x * x)[:4], axis=0, keepdims=True)
    return row, split3(x), split3(norm)


def by_half(row, low, high):
    return jnp.where(row < 4, low, high)


def by_row(row, values, rest):
    for i, value in reversed(list(enumerate(values))):
        rest = jnp.where(row == i, value, rest)
    return rest


def source_features(x):
    row, (high, middle, low), norm = doubled(x)
    ones = jnp.where(row < 6, 1.0, 0.0)
    groups = [high, by_half(row, high, middle), by_half(row, middle, low), by_row(row, norm, ones)]
    return jnp.concatenate(groups, 0)


def target_features(x):
    row, (high, middle, low), norm = doubled(x)
    weight = jnp.where((row & 3) < 3, -2.0, 2.0)
    groups = [by_half(row, high, middle), by_half(row, low, high), by_half(row, middle, high)]
    last = by_row(row, (1.0, 1.0, 1.0) + norm, 0.0)
    return jnp.concatenate([g * weight for g in groups] + [last], 0)


def pack_kernel(t_position, t_vector, t_radius, *refs):
    position, vector, radius, current, incidence, excitation, block, copies, ports = refs
    count = t_radius.shape[1]
    rows = [t_position[...] - MIDDLE, t_radius[...], t_vector[...], jnp.zeros((1, count), F32)]
    wide = [jnp.concatenate(rows, 0), jnp.zeros((8, LANES - count), F32)]
    block[...] = jnp.concatenate(wide, 1)
    sources = copies.at[0]
    for r in range(8):
        here = slice(r * LANES, (r + 1) * LANES)
        for q in range(3):
            sources[8 * q + r : 8 * q + r + 1, :] = position[q : q + 1, here] - MIDDLE
            sources[8 * q + r + 32 : 8 * q + r + 33, :] = vector[q : q + 1, here]
    sources[24:32, :] = radius[...]
    sources[56:64, :] = current[...]
    sources[64:72, :] = incidence[...].astype(F32)
    for i in range(1, copies.shape[0]):
        copies[i] = copies[0]
    ports[...] = jnp.transpose(jnp.broadcast_to(excitation[...].astype(F32), ports.shape))


def pack(shapes, *arrays):
    vmem = pl.BlockSpec(memory_space=pltpu.VMEM)
    return pl.pallas_call(
        pack_kernel,
        out_shape=[jax.ShapeDtypeStruct(shape, F32) for shape in shapes],
        in_specs=[vmem] * len(arrays),
        out_specs=[vmem] * len(shapes),
        name="pack",
    )(*arrays)


def prepare_targets(pairs, squared, vectors):
    for j in range(len(FLIPS)):
        here = slice(2 * j * COUNT, 2 * (j + 1) * COUNT)
        x = jnp.concatenate([pairs[j][0][:, :COUNT], pairs[j][1][:, :COUNT]], 1)
        squared[here, :] = jnp.transpose(target_features(x)).astype(BF16)
        for d in range(3):
            vectors[d, here, :] = jnp.transpose(
                jnp.broadcast_to(x[4 + d : 5 + d, :], (2 * COUNT, LANES))
            )


def add_sources(sources, ports, squared, vectors, total, even, odd):
    port = ports[...]
    blocks = sources.shape[0]

    def prepare(b, features, currents):
        for r in range(WIDTH // LANES):
            here = slice(r * LANES, (r + 1) * LANES)
            x = sources[b, pl.ds(r, 8, stride=8), :]
            features[:, here] = source_features(x).astype(BF16)
            current = sources[b, pl.ds(56 + r, 1), :]
            incidence = sources[b, pl.ds(64 + r, 1), :]
            matched = jnp.where(port == incidence, current, 0.0)
            currents[here, :] = jnp.transpose(matched).astype(BF16)

    def inductance(b, k, features):
        these = slice(k * TILE, (k + 1) * TILE)
        distance = jnp.dot(squared[...], features[:, these], preferred_element_type=F32)
        alignment = []
        for r in range(k * TILE // LANES, (k + 1) * TILE // LANES):
            x, y, z = (sources[b, pl.ds(8 * d + r, 1), :] for d in (4, 5, 6))
            alignment.append(vectors[0] * x + vectors[1] * y + vectors[2] * z)
        return (jnp.concatenate(alignment, 1) * lax.rsqrt(distance)).astype(BF16)

    def add(b, features, currents):
        for k in range(WIDTH // TILE):
            these = slice(k * TILE, (k + 1) * TILE)
            total[...] += jnp.dot(
                inductance(b, k, features), currents[these, :], preferred_element_type=F32
            )

    prepare(0, *even)

    def some(i, carry):
        for j in range(UNROLL):
            b = UNROLL * i + j
            this, other = (even, odd) if j % 2 == 0 else (odd, even)
            prepare(jnp.minimum(b + 1, blocks - 1), *other)
            add(b, *this)
        return carry

    lax.fori_loop(0, blocks // UNROLL, some, 0)


def near_kernel(*refs):
    pairs, refs = refs[: len(FLIPS)], refs[len(FLIPS) :]
    sources, ports, squared, vectors, total, *buffers = refs
    prepare_targets(pairs, squared, vectors)
    total[...] = jnp.zeros_like(total)
    add_sources(sources, ports, squared, vectors, total, buffers[:2], buffers[2:])


def far_kernel(sources, ports, squared, vectors, start, keep, send, total, *buffers):
    total[...] = start[...]
    add_sources(sources, ports, squared, vectors, total, buffers[:2], buffers[2:])
    for j in range(len(FLIPS)):
        here = slice(j * COUNT, (j + 1) * COUNT)
        keep[here, :] = total[2 * j * COUNT : (2 * j + 1) * COUNT, :]
        send[here, :] = total[(2 * j + 1) * COUNT : 2 * (j + 1) * COUNT, :]


ROWS = 2 * len(FLIPS) * COUNT
BUFFERS = [pltpu.VMEM((DEPTH, WIDTH), BF16), pltpu.VMEM((WIDTH, LANES), BF16)] * 2


def options(sources):
    pairs = ROWS * sources.shape[0] * WIDTH
    return {
        "compiler_params": pltpu.CompilerParams(vmem_limit_bytes=24 * 2**20),
        "cost_estimate": pl.CostEstimate(
            flops=2 * pairs * (DEPTH + LANES), bytes_accessed=2**21, transcendentals=pairs
        ),
    }


def near_volts(pairs, sources, ports):
    vmem = pl.BlockSpec(memory_space=pltpu.VMEM)
    return pl.pallas_call(
        near_kernel,
        out_shape=[
            jax.ShapeDtypeStruct((ROWS, DEPTH), BF16),
            jax.ShapeDtypeStruct((3, ROWS, LANES), F32),
            jax.ShapeDtypeStruct((ROWS, LANES), F32),
        ],
        in_specs=[vmem] * (len(FLIPS) + 2),
        out_specs=[vmem] * 3,
        scratch_shapes=BUFFERS,
        name="near_volts",
        **options(sources),
    )(*pairs, sources, ports)


def far_volts(sources, ports, squared, vectors, start):
    vmem = pl.BlockSpec(memory_space=pltpu.VMEM)
    return pl.pallas_call(
        far_kernel,
        out_shape=[jax.ShapeDtypeStruct((ROWS // 2, LANES), F32)] * 2,
        in_specs=[vmem] * 5,
        out_specs=[vmem] * 2,
        scratch_shapes=[pltpu.VMEM((ROWS, LANES), F32)] + BUFFERS,
        name="far_volts",
        **options(sources),
    )(sources, ports, squared, vectors, start)


def per_device(
    target_position,
    target_vector,
    target_radius,
    source_position,
    source_vector,
    source_radius,
    source_current,
    incidence,
    excitation,
):
    plane = SHAPE[0] * SHAPE[1]
    block, copies, ports = pack(
        [(8, LANES), (plane, 72, LANES), (LANES, LANES)],
        target_position,
        target_vector,
        target_radius[None],
        source_position,
        source_vector,
        source_radius.reshape(8, LANES),
        source_current.reshape(8, LANES),
        incidence.reshape(8, LANES),
        excitation[None],
    )
    swap = [(0, 1), (1, 0)]
    other = lax.ppermute(block, "c", swap)
    sources = lax.all_to_all(copies, ("y", "x"), 0, 0, tiled=True)
    pair = jnp.stack([block, other])
    zh = range(SHAPE[2])
    pairs = [pair] + [lax.ppermute(pair, "zh", [(i, i ^ k) for i in zh]) for k in FLIPS[1:]]
    sources, pairs = lax.optimization_barrier((sources, pairs))
    far = lax.ppermute(sources, "zl", swap)
    prepared = near_volts(pairs, sources, ports)
    keep, send = far_volts(far, ports, *prepared)
    partial = (keep + lax.ppermute(send, "c", swap)).reshape(len(FLIPS), COUNT, LANES)
    shares = [partial[0]]
    for j, k in enumerate(FLIPS[1:], 1):
        shares.append(lax.ppermute(partial[j], "zh", [(i, i ^ k) for i in zh]))
    return sum(shares[1:], shares[0])


def solution(mesh):
    fine = Mesh(mesh.devices.reshape(SHAPE), AXES)
    placed = (P(None, AXES), P(None, AXES), P(AXES), P(None, AXES), P(None, AXES))
    placed += (P(AXES), P(AXES), P(AXES), P())
    return jax.shard_map(
        per_device, mesh=fine, in_specs=placed, out_specs=P(AXES, None), check_vma=False
    )
```

```python
import jax
import jax.numpy as jnp
from jax import lax
from jax.experimental import pallas as pl
from jax.experimental.pallas import tpu as pltpu
from jax.sharding import Mesh, PartitionSpec as P

BF16 = jnp.bfloat16
F32 = jnp.float32
TILE = 256
UNROLL = 16
DEPTH = 32
LANES = 128
MIDDLE = 2.0
COUNT = 64
WIDTH = 1024
AXES = ("y", "x", "zh", "zl", "c")
SHAPE = (4, 4, 4, 2, 2)
FLIPS = (0, 2, 1, 3)


def split3(x):
    high = x.astype(BF16).astype(F32)
    rest = x - high
    middle = rest.astype(BF16).astype(F32)
    low = (rest - middle).astype(BF16).astype(F32)
    return high, middle, low


def doubled(x):
    row = lax.broadcasted_iota(jnp.int32, x.shape, 0)
    x = jnp.concatenate([x[:4], x[:4]], 0)
    norm = jnp.sum((x * x)[:4], axis=0, keepdims=True)
    return row, split3(x), split3(norm)


def by_half(row, low, high):
    return jnp.where(row < 4, low, high)


def by_row(row, values, rest):
    for i, value in reversed(list(enumerate(values))):
        rest = jnp.where(row == i, value, rest)
    return rest


def source_features(x):
    row, (high, middle, low), norm = doubled(x)
    ones = jnp.where(row < 6, 1.0, 0.0)
    groups = [high, by_half(row, high, middle), by_half(row, middle, low), by_row(row, norm, ones)]
    return jnp.concatenate(groups, 0)


def target_features(x):
    row, (high, middle, low), norm = doubled(x)
    weight = jnp.where((row & 3) < 3, -2.0, 2.0)
    groups = [by_half(row, high, middle), by_half(row, low, high), by_half(row, middle, high)]
    last = by_row(row, (1.0, 1.0, 1.0) + norm, 0.0)
    return jnp.concatenate([g * weight for g in groups] + [last], 0)


def pack_kernel(t_position, t_vector, t_radius, *refs):
    position, vector, radius, current, incidence, excitation, block, copies, ports = refs
    count = t_radius.shape[1]
    rows = [t_position[...] - MIDDLE, t_radius[...], t_vector[...], jnp.zeros((1, count), F32)]
    wide = [jnp.concatenate(rows, 0), jnp.zeros((8, LANES - count), F32)]
    block[...] = jnp.concatenate(wide, 1)
    sources = copies.at[0]
    for r in range(8):
        here = slice(r * LANES, (r + 1) * LANES)
        for q in range(3):
            sources[8 * q + r : 8 * q + r + 1, :] = position[q : q + 1, here] - MIDDLE
            sources[8 * q + r + 32 : 8 * q + r + 33, :] = vector[q : q + 1, here]
    sources[24:32, :] = radius[...]
    sources[56:64, :] = current[...]
    sources[64:72, :] = incidence[...].astype(F32)
    for i in range(1, copies.shape[0]):
        copies[i] = copies[0]
    ports[...] = jnp.transpose(jnp.broadcast_to(excitation[...].astype(F32), ports.shape))


def pack(shapes, *arrays):
    vmem = pl.BlockSpec(memory_space=pltpu.VMEM)
    return pl.pallas_call(
        pack_kernel,
        out_shape=[jax.ShapeDtypeStruct(shape, F32) for shape in shapes],
        in_specs=[vmem] * len(arrays),
        out_specs=[vmem] * len(shapes),
        name="pack",
    )(*arrays)


def prepare_targets(pairs, squared, vectors):
    for j in range(2 * len(FLIPS)):
        here = slice(j * COUNT, (j + 1) * COUNT)
        x = pairs[j % len(FLIPS)][j // len(FLIPS)]
        squared[here, :] = jnp.transpose(target_features(x))[:COUNT].astype(BF16)
        for d in range(3):
            spread = jnp.broadcast_to(x[4 + d : 5 + d, :], (LANES, LANES))
            vectors[d, here, :] = jnp.transpose(spread)[:COUNT]


def add_sources(sources, ports, squared, vectors, total, even, odd):
    port = ports[...]
    blocks = sources.shape[0]

    def prepare(b, features, currents):
        for r in range(WIDTH // LANES):
            here = slice(r * LANES, (r + 1) * LANES)
            x = sources[b, pl.ds(r, 8, stride=8), :]
            features[:, here] = source_features(x).astype(BF16)
            current = sources[b, pl.ds(56 + r, 1), :]
            incidence = sources[b, pl.ds(64 + r, 1), :]
            matched = jnp.where(port == incidence, current, 0.0)
            currents[here, :] = jnp.transpose(matched).astype(BF16)

    def inductance(b, k, features):
        these = slice(k * TILE, (k + 1) * TILE)
        distance = jnp.dot(squared[...], features[:, these], preferred_element_type=F32)
        alignment = []
        for r in range(k * TILE // LANES, (k + 1) * TILE // LANES):
            x, y, z = (sources[b, pl.ds(8 * d + r, 1), :] for d in (4, 5, 6))
            alignment.append(vectors[0] * x + vectors[1] * y + vectors[2] * z)
        return (jnp.concatenate(alignment, 1) * lax.rsqrt(distance)).astype(BF16)

    def add(b, features, currents):
        for k in range(WIDTH // TILE):
            these = slice(k * TILE, (k + 1) * TILE)
            total[...] += jnp.dot(
                inductance(b, k, features), currents[these, :], preferred_element_type=F32
            )

    prepare(0, *even)

    def some(i, carry):
        for j in range(UNROLL):
            b = UNROLL * i + j
            this, other = (even, odd) if j % 2 == 0 else (odd, even)
            prepare(jnp.minimum(b + 1, blocks - 1), *other)
            add(b, *this)
        return carry

    lax.fori_loop(0, blocks // UNROLL, some, 0)


def near_kernel(*refs):
    pairs, refs = refs[: len(FLIPS)], refs[len(FLIPS) :]
    sources, ports, squared, vectors, total, *buffers = refs
    prepare_targets(pairs, squared, vectors)
    total[...] = jnp.zeros_like(total)
    add_sources(sources, ports, squared, vectors, total, buffers[:2], buffers[2:])


def far_kernel(sources, ports, squared, vectors, start, keep, send, total, *buffers):
    total[...] = start[...]
    add_sources(sources, ports, squared, vectors, total, buffers[:2], buffers[2:])
    half = total.shape[0] // 2
    keep[...] = total[:half, :]
    send[...] = total[half:, :]


ROWS = 2 * len(FLIPS) * COUNT
BUFFERS = [pltpu.VMEM((DEPTH, WIDTH), BF16), pltpu.VMEM((WIDTH, LANES), BF16)] * 2


def options(sources):
    pairs = ROWS * sources.shape[0] * WIDTH
    return {
        "compiler_params": pltpu.CompilerParams(vmem_limit_bytes=24 * 2**20),
        "cost_estimate": pl.CostEstimate(
            flops=2 * pairs * (DEPTH + LANES), bytes_accessed=2**21, transcendentals=pairs
        ),
    }


def near_volts(pairs, sources, ports):
    vmem = pl.BlockSpec(memory_space=pltpu.VMEM)
    return pl.pallas_call(
        near_kernel,
        out_shape=[
            jax.ShapeDtypeStruct((ROWS, DEPTH), BF16),
            jax.ShapeDtypeStruct((3, ROWS, LANES), F32),
            jax.ShapeDtypeStruct((ROWS, LANES), F32),
        ],
        in_specs=[vmem] * (len(FLIPS) + 2),
        out_specs=[vmem] * 3,
        scratch_shapes=BUFFERS,
        name="near_volts",
        **options(sources),
    )(*pairs, sources, ports)


def far_volts(sources, ports, squared, vectors, start):
    vmem = pl.BlockSpec(memory_space=pltpu.VMEM)
    return pl.pallas_call(
        far_kernel,
        out_shape=[jax.ShapeDtypeStruct((ROWS // 2, LANES), F32)] * 2,
        in_specs=[vmem] * 5,
        out_specs=[vmem] * 2,
        scratch_shapes=[pltpu.VMEM((ROWS, LANES), F32)] + BUFFERS,
        name="far_volts",
        **options(sources),
    )(sources, ports, squared, vectors, start)


def per_device(
    target_position,
    target_vector,
    target_radius,
    source_position,
    source_vector,
    source_radius,
    source_current,
    incidence,
    excitation,
):
    plane = SHAPE[0] * SHAPE[1]
    block, copies, ports = pack(
        [(8, LANES), (plane, 72, LANES), (LANES, LANES)],
        target_position,
        target_vector,
        target_radius[None],
        source_position,
        source_vector,
        source_radius.reshape(8, LANES),
        source_current.reshape(8, LANES),
        incidence.reshape(8, LANES),
        excitation[None],
    )
    swap = [(0, 1), (1, 0)]
    other = lax.ppermute(block, "c", swap)
    sources = lax.all_to_all(copies, ("y", "x"), 0, 0, tiled=True)
    pair = jnp.stack([block, other])
    zh = range(SHAPE[2])
    pairs = [pair] + [lax.ppermute(pair, "zh", [(i, i ^ k) for i in zh]) for k in FLIPS[1:]]
    sources, pairs = lax.optimization_barrier((sources, pairs))
    far = lax.ppermute(sources, "zl", swap)
    prepared = near_volts(pairs, sources, ports)
    keep, send = far_volts(far, ports, *prepared)
    partial = (keep + lax.ppermute(send, "c", swap)).reshape(len(FLIPS), COUNT, LANES)
    shares = [partial[0]]
    for j, k in enumerate(FLIPS[1:], 1):
        shares.append(lax.ppermute(partial[j], "zh", [(i, i ^ k) for i in zh]))
    return sum(shares[1:], shares[0])


def solution(mesh):
    fine = Mesh(mesh.devices.reshape(SHAPE), AXES)
    placed = (P(None, AXES), P(None, AXES), P(AXES), P(None, AXES), P(None, AXES))
    placed += (P(AXES), P(AXES), P(AXES), P())
    return jax.shard_map(
        per_device, mesh=fine, in_specs=placed, out_specs=P(AXES, None), check_vma=False
    )
```
